32 devices in a mesh: groups: 2 (over y), row: 4 (over z), col: 4 (over x, core).
Axes of the slice: x: 2, y: 2, z: 4, core: 2. Of those that a mesh axis runs over, the one named last changes fastest.
Arguments:
- activations: bfloat16 [1024, 8192], P(('groups', 'row'), 'col'), parts along dimension 0, may hold values from -6 to 6
- w_gate: bfloat16 [8192, 14336], P('row', 'col'), may hold values from -0.0625 to 0.0625
- w_up: bfloat16 [8192, 14336], P('row', 'col'), may hold values from -0.0625 to 0.0625
- w_down: bfloat16 [8192, 14336], P('row', 'col'), may hold values from -0.1875 to 0.1875
- block_lists: int32 [4, 4, 2], P('groups'), parts along dimension 0, may hold values from 0 to 28, as said below
Outputs:
- ffn_output: bfloat16 [1024, 8192], P(('groups', 'row'), 'col'), parts along dimension 0
The draws below stay inside these ranges and needn't reach their ends.
There are 2 independent parts, one for each index of `groups`. The reference program is written for one: setup_inputs(seed, part) draws one part's arguments, and reference() takes and returns one part's arrays. A program takes and returns all parts, laid end to end along the dimension named above; an argument that names none is the same for every part. Nothing has to cross between parts.
Inputs may be any that keep to these rules, and one draw needn't show every extreme that they name: block_lists[b, c, 0] is a block of slab c; block_lists[b, c, 1] is another block of the same slab, or S = 14336 // (128 * 4) meaning none; some token block uses both entries of some slab.
All inputs are finite; a program needn't handle non-finite values.
Results may differ from the reference program's by a relative error of at most 0.011.
Values may be sent and summed in bfloat16 or wider, within the bound.
A program may use at most 192 MiB of HBM per device.

```python
import jax
import jax.numpy as jnp
from jax import lax

D = 8192
FF = 14336
TBLK = 256
TOKENS = 512
TBLOCKS = 2
N_COL = 4


def draw_block_lists(key, part):
    key = jax.random.fold_in(key, 7)
    key_list = jax.random.split(key, 4)
    slab_blocks = FF // 128 // N_COL
    block_shape = (TBLOCKS, N_COL)
    first_block = jax.random.randint(key_list[0], block_shape, 0, slab_blocks)
    offset_draw = jax.random.randint(key_list[1], block_shape, 1, slab_blocks)
    second_block = (first_block + offset_draw) % slab_blocks
    chance_draw = jax.random.randint(key_list[2], block_shape, 0, 10)
    forced = jax.random.randint(key_list[3], (), 0, TBLOCKS * N_COL)
    flat_ids = jnp.arange(TBLOCKS * N_COL, dtype=jnp.int32).reshape(block_shape)
    keep_second = (chance_draw < 6) | (flat_ids == forced)
    second_block = jnp.where(keep_second, second_block, slab_blocks)
    return jnp.stack([first_block, second_block], axis=-1).astype(jnp.int32)


def level_of(stream_key, shape, pieces, smallest, top_value):
    level = 1.0
    for dim, shards_of in pieces:
        steps = jax.random.uniform(jax.random.fold_in(jax.random.fold_in(stream_key, 6), dim), (shards_of,), jnp.float32, smallest / len(pieces), top_value / len(pieces))
        level = level * jnp.repeat(jnp.exp(steps), shape[dim] // shards_of).reshape((-1,) + (1,) * (len(shape) - 1 - dim))
    return level


def bell_draw(key, dims, scale, limit, cuts=(), kind=jnp.bfloat16):
    gain = level_of(key, dims, cuts, -0.22, 0.18) if cuts else 1.0
    result = jax.random.normal(key, dims, jnp.float32) * scale * gain
    return jnp.minimum(jnp.maximum(result, -limit), limit).astype(kind)


def setup_inputs(seed: int = 0, part: int = 0) -> dict:
    seeds = jax.random.split(jax.random.key(seed), 6)
    part_keys = jax.random.split(jax.random.fold_in(seeds[5], part), 6)
    return {
        "activations": bell_draw(part_keys[0], (TOKENS, D), 1.0, 6.0, ((0, 4), (1, 4))),
        "w_gate": bell_draw(seeds[1], (D, FF), D ** -0.5, 0.0625, ((0, 4), (1, 4))),
        "w_up": bell_draw(seeds[2], (D, FF), D ** -0.5, 0.0625, ((0, 4), (1, 4))),
        "w_down": bell_draw(seeds[3], (D, FF), (256 * N_COL) ** -0.5, 0.1875, ((0, 4), (1, 4))),
        "block_lists": draw_block_lists(jax.random.fold_in(jax.random.fold_in(seeds[5], part), 71), part),
    }


def reference(activations, w_gate, w_up, w_down, block_lists):
    width = 128
    slab_blocks = FF // width // N_COL
    slots_all = 2 * N_COL
    token_blocks = activations.reshape(TBLOCKS, TBLK, D)
    slab_ids = jnp.arange(N_COL, dtype=jnp.int32)[:, None]
    offsets = jnp.arange(width, dtype=jnp.int32)

    def one_block(pair):
        token_rows, lists = pair
        live_flag = (lists < slab_blocks).astype(jnp.float32).reshape(slots_all)
        chosen = (slab_ids * slab_blocks + jnp.minimum(lists, slab_blocks - 1)).reshape(slots_all)
        column_ids = (chosen[:, None] * width + offsets[None, :]).reshape(slots_all * width).astype(jnp.int32)
        gate_value = jnp.dot(token_rows, jnp.take(w_gate, column_ids, axis=1), preferred_element_type=jnp.float32)
        up_value = jnp.dot(token_rows, jnp.take(w_up, column_ids, axis=1), preferred_element_type=jnp.float32)
        mask_row = jnp.repeat(live_flag, width)
        hidden = (jax.nn.relu(gate_value) * up_value * mask_row[None, :]).astype(jnp.bfloat16)
        down_cols = jnp.take(w_down, column_ids, axis=1).reshape(D, slots_all, width)
        hidden_slots = hidden.reshape(TBLK, slots_all, width)

        def add_slot(total, slot_index):
            hidden_piece = lax.dynamic_index_in_dim(hidden_slots, slot_index, 1, False)
            down_piece = lax.dynamic_index_in_dim(down_cols, slot_index, 1, False)
            term = lax.dot_general(hidden_piece, down_piece, (((1,), (1,)), ((), ())), preferred_element_type=jnp.float32)
            rounded = lax.optimization_barrier(term.astype(jnp.bfloat16))
            return total + rounded.astype(jnp.float32), None

        total, _ = lax.scan(add_slot, jnp.zeros((TBLK, D), jnp.float32), jnp.arange(slots_all, dtype=jnp.int32))
        return total

    summed = lax.map(one_block, (token_blocks, block_lists))
    return summed.reshape(TOKENS, D).astype(jnp.bfloat16)
```

```python
import functools

import jax
import jax.numpy as jnp
from jax import lax
from jax.experimental import pallas as pl
from jax.experimental.pallas import tpu as pltpu
from jax.sharding import PartitionSpec as P

WIDTH = 128
PARTS = 2


def partner_2(block, axis, stride):
    count = lax.axis_size(axis)
    route = []
    for low in range(count):
        high = low | 1 << stride
        if high != low and high < count:
            route += [(low, high), (high, low)]
    return lax.ppermute(block, axis, route)


def general_shards(activations, w_gate, w_up, w_down, block_lists):
    row_count = lax.axis_size("row")
    row_id = lax.axis_index("row")
    col_id = lax.axis_index("col")
    slab_blocks = w_gate.shape[1] // WIDTH
    gathered = lax.all_gather(activations, "col", axis=1, tiled=True)
    partner = partner_2(gathered, "row", 0)
    wanted = lax.dynamic_index_in_dim(block_lists, col_id, axis=1, keepdims=False).reshape(
        row_count
    )
    chosen = jnp.minimum(wanted, slab_blocks - 1)
    own_entry = lax.dynamic_index_in_dim(wanted, row_id, axis=0, keepdims=False)
    live_flag = (own_entry < slab_blocks).astype(jnp.float32)

    def fetch(weight):
        pieces = weight.reshape(weight.shape[0], slab_blocks, WIDTH)
        outgoing = jnp.take(pieces, chosen, axis=1)
        got = lax.all_to_all(outgoing, "row", split_axis=1, concat_axis=0, tiled=True)
        return got.reshape(got.shape[0], WIDTH)

    gate_cols, up_cols, down_cols = fetch(w_gate), fetch(w_up), fetch(w_down)

    def term_of(token_rows):
        gate_value = jnp.dot(token_rows, gate_cols, preferred_element_type=jnp.float32)
        up_value = jnp.dot(token_rows, up_cols, preferred_element_type=jnp.float32)
        hidden = (jax.nn.relu(gate_value) * up_value * live_flag).astype(jnp.bfloat16)
        return lax.dot_general(
            hidden, down_cols, (((1,), (1,)), ((), ())), preferred_element_type=jnp.float32
        ).astype(jnp.bfloat16)

    own = term_of(gathered)
    received = partner_2(term_of(partner), "row", 0)
    own_sum, other_sum = (
        lax.psum_scatter(term, "col", scatter_dimension=1, tiled=True).astype(jnp.float32)
        for term in (own, received)
    )
    return (own_sum + other_sum).astype(jnp.bfloat16)


def pick_kernel(lists, col, gate, up, down, gate_out, up_out, down_out):
    gate_out[0] = gate[...]
    up_out[0] = up[...]
    down_out[0] = down[...]


def pick(block_lists, col_id, w_gate, w_up, w_down):
    depth, slab = w_gate.shape
    blocks = block_lists.shape[0]
    top = slab // WIDTH - 1

    def chosen(b, s, lists, col):
        return 0, jnp.minimum(lists[b, col[0], s], top)

    shape = jax.ShapeDtypeStruct((blocks, depth, 2 * WIDTH), w_gate.dtype)
    return pl.pallas_call(
        pick_kernel,
        grid_spec=pltpu.PrefetchScalarGridSpec(
            num_scalar_prefetch=2,
            grid=(blocks, 2),
            in_specs=[pl.BlockSpec((depth, WIDTH), chosen)] * 3,
            out_specs=[pl.BlockSpec((1, depth, WIDTH), lambda b, s, lists, col: (b, 0, s))] * 3,
        ),
        out_shape=[shape] * 3,
        compiler_params=pltpu.CompilerParams(vmem_limit_bytes=32 * 2**20),
    )(block_lists, col_id, w_gate, w_up, w_down)


def layer_kernel(
    slab_blocks, lists, act, w_gate, w_up, w_down, out,
    gate_w, up_w, down_w, x_all, part_f32, part_out, part_in, hid_all,
    term, term_in, half_out, half_in, sum_out,
    w_sem, a_send, a_recv, g1_send, g1_recv, g2_send, g2_recv, g3_send, g3_recv,
    p_send, p_recv, h_send, h_recv, t_send, t_recv, s_send, s_recv, o_send, o_recv,
):
    parts, rows, cols, size, depth = x_all.shape
    blocks = rows // 2
    toks = cols * size
    r, c = lax.axis_index("row"), lax.axis_index("col")
    core, chip = c % 2, c // 2
    c1 = c + 1 - 2 * core
    c2 = (c + 2) % 4
    c3 = (c1 + 2) % 4

    loads = [
        pltpu.make_async_copy(w_gate, gate_w, w_sem.at[0]),
        pltpu.make_async_copy(w_up, up_w, w_sem.at[1]),
        pltpu.make_async_copy(w_down, down_w, w_sem.at[2]),
    ]
    for load in loads:
        load.start()

    barrier = pltpu.get_barrier_semaphore()
    for dr in range(rows):
        for dc in range(cols):
            if dr or dc:
                pl.semaphore_signal(
                    barrier, inc=1,
                    device_id={"row": (r + dr) % rows, "col": (c + dc) % cols},
                    device_id_type=pl.DeviceIdType.MESH,
                )
    pl.semaphore_wait(barrier, rows * cols - 1)

    drains = []

    def remote(src, dst, send, recv, row, col):
        return pltpu.make_async_remote_copy(
            src_ref=src, dst_ref=dst, send_sem=send, recv_sem=recv,
            device_id={"row": row, "col": col}, device_id_type=pl.DeviceIdType.MESH,
        )

    def send_to(src, dst, send, recv, row, col):
        copy = remote(src, dst, send, recv, row, col)
        copy.start()
        drains.append((None, copy))

    def send_or_keep(src, dst, send, recv, row, col):
        other = jnp.logical_or(row != r, col != c)
        copy = remote(src, dst, send, recv, row, col)

        @pl.when(other)
        def _():
            copy.start()

        @pl.when(jnp.logical_not(other))
        def _():
            pltpu.make_async_copy(src, dst, recv).start()

        drains.append((other, copy))

    def arrived(dst, recv):
        pltpu.make_async_copy(dst, dst, recv).wait()

    def spread(p):
        for q in range(cols):
            send_or_keep(
                act.at[pl.ds((p * cols + q) * size, size)], x_all.at[p, r, q],
                a_send.at[p, q], a_recv.at[p, r], c, q,
            )

    def forward(p):
        for k in range(rows):
            s = (r + k) % rows
            piece = x_all.at[p, s, c]
            arrived(piece, a_recv.at[p, s])
            send_to(piece, piece, g2_send.at[p, k], g2_recv.at[p, s], r, c2)
            send_to(piece, piece, g1_send.at[p, k], g1_recv.at[p, s], r, c1)

    def forward_again(p):
        for k in range(rows):
            s = (r + k) % rows
            piece = x_all.at[p, s, c2]
            arrived(piece, g2_recv.at[p, s])
            send_to(piece, piece, g3_send.at[p, k], g3_recv.at[p, s], r, c1)

    def collected(p):
        for s in range(rows):
            arrived(x_all.at[p, s, c1], g1_recv.at[p, s])
        for s in range(rows):
            arrived(x_all.at[p, s, c3], g3_recv.at[p, s])

    def gate_up(p):
        for b in range(blocks):
            x = x_all[p, 2 * b : 2 * b + 2].reshape(2 * toks, depth)
            for j, weight in enumerate((gate_w, up_w)):
                value = jnp.dot(x, weight[b], preferred_element_type=jnp.float32)
                value = value.reshape(2, toks, 2 * WIDTH)
                lanes = slice(j * 2 * WIDTH, (j + 1) * 2 * WIDTH)
                part_f32[p, 2 * b : 2 * b + 2, :, lanes] = value
                part_out[p, 2 * b : 2 * b + 2, :, lanes] = value.astype(jnp.bfloat16)
        for k in range(1, rows):
            s = (r + k) % rows
            send_to(part_out.at[p, s], part_in.at[p, k - 1], p_send.at[p, k], p_recv.at[p, k], s, c)

    def hidden(p):
        total = part_f32[p, r]
        for k in range(1, rows):
            arrived(part_in.at[p, k - 1], p_recv.at[p, k])
            total = total + part_in[p, k - 1].astype(jnp.float32)
        value = jnp.maximum(total[:, : 2 * WIDTH], 0.0) * total[:, 2 * WIDTH :]
        live = [jnp.where(lists[r // 2, c, s] < slab_blocks, 1.0, 0.0) for s in range(2)]
        lane = lax.broadcasted_iota(jnp.int32, value.shape, 1)
        value = value * jnp.where(lane < WIDTH, live[0], live[1])
        hid_all[p, r] = value.astype(jnp.bfloat16)
        for k in range(1, rows):
            mine = hid_all.at[p, r]
            send_to(mine, mine, h_send.at[p, k], h_recv.at[p, k], (r + k) % rows, c)

    def down(p):
        for k in range(1, rows):
            arrived(hid_all.at[p, (r + rows - k) % rows], h_recv.at[p, k])
        tile = 512
        for b in range(blocks):
            h = hid_all[p, 2 * b : 2 * b + 2].reshape(2 * toks, 2 * WIDTH)
            for n in range(0, depth, tile):
                value = lax.dot_general(
                    h, down_w[b, n : n + tile], (((1,), (1,)), ((), ())),
                    preferred_element_type=jnp.float32,
                ).astype(jnp.bfloat16)
                for i in range(2):
                    for q in range(cols):
                        at = (i * cols + q) * size
                        term[p, q % 2, q // 2, 2 * b + i, :, n : n + tile] = value[at : at + size]
        send_to(term.at[p, 1 - core], term_in.at[p], t_send.at[p], t_recv.at[p], r, c1)

    def pair(p):
        arrived(term_in.at[p], t_recv.at[p])
        for k in range(rows):
            s = (r + k) % rows
            value = term[p, core, 1 - chip, s].astype(jnp.float32)
            value = value + term_in[p, 1 - chip, s].astype(jnp.float32)
            half_out[p, s] = value.astype(jnp.bfloat16)
            send_to(half_out.at[p, s], half_in.at[p, s], s_send.at[p, k], s_recv.at[p, s], r, c2)

    def finish(p):
        for k in range(rows):
            s = (r + k) % rows
            value = term[p, core, chip, s].astype(jnp.float32)
            value = value + term_in[p, chip, s].astype(jnp.float32)
            arrived(half_in.at[p, s], s_recv.at[p, s])
            value = value + half_in[p, s].astype(jnp.float32)
            sum_out[p, s] = value.astype(jnp.bfloat16)
            send_or_keep(
                sum_out.at[p, s], out.at[pl.ds((p * cols + c) * size, size)],
                o_send.at[p, k], o_recv.at[p, c], s, r,
            )

    for p in range(parts):
        spread(p)
    forward(0)
    forward_again(0)
    forward(1)
    collected(0)
    loads[0].wait()
    loads[1].wait()
    gate_up(0)
    forward_again(1)
    collected(1)
    gate_up(1)
    hidden(0)
    loads[2].wait()
    down(0)
    hidden(1)
    pair(0)
    down(1)
    finish(0)
    pair(1)
    finish(1)
    for p in range(parts):
        for q in range(cols):
            arrived(out.at[pl.ds((p * cols + q) * size, size)], o_recv.at[p, q])
    for other, copy in drains:
        if other is None:
            copy.wait_send()
        else:
            pl.when(other)(copy.wait_send)


def layer(block_lists, activations, gate, up, down, rows, cols, slab_blocks):
    tokens, depth = activations.shape
    size = tokens // (PARTS * cols)
    toks = cols * size
    bf16, f32 = jnp.bfloat16, jnp.float32
    sem = pltpu.SemaphoreType.DMA
    by_row, by_col = sem((PARTS, rows)), sem((PARTS, cols))
    return pl.pallas_call(
        functools.partial(layer_kernel, slab_blocks),
        out_shape=jax.ShapeDtypeStruct(activations.shape, bf16),
        in_specs=[pl.BlockSpec(memory_space=pltpu.SMEM)] + [pl.BlockSpec(memory_space=pl.ANY)] * 4,
        out_specs=pl.BlockSpec(memory_space=pltpu.VMEM),
        scratch_shapes=[
            pltpu.VMEM(gate.shape, bf16),
            pltpu.VMEM(up.shape, bf16),
            pltpu.VMEM(down.shape, bf16),
            pltpu.VMEM((PARTS, rows, cols, size, depth), bf16),
            pltpu.VMEM((PARTS, rows, toks, 4 * WIDTH), f32),
            pltpu.VMEM((PARTS, rows, toks, 4 * WIDTH), bf16),
            pltpu.VMEM((PARTS, rows - 1, toks, 4 * WIDTH), bf16),
            pltpu.VMEM((PARTS, rows, toks, 2 * WIDTH), bf16),
            pltpu.VMEM((PARTS, 2, 2, rows, size, depth), bf16),
            pltpu.VMEM((PARTS, 2, rows, size, depth), bf16),
            pltpu.VMEM((PARTS, rows, size, depth), bf16),
            pltpu.VMEM((PARTS, rows, size, depth), bf16),
            pltpu.VMEM((PARTS, rows, size, depth), bf16),
            sem((3,)),
            by_col, by_row,
            by_row, by_row, by_row, by_row, by_row, by_row,
            by_row, by_row, by_row, by_row,
            sem((PARTS,)), sem((PARTS,)),
            by_row, by_row, by_row, by_col,
        ],
        compiler_params=pltpu.CompilerParams(
            collective_id=0, has_side_effects=True, vmem_limit_bytes=48 * 2**20
        ),
    )(block_lists, activations, gate, up, down)


def near_shards(rows, cols, activations, w_gate, w_up, w_down, block_lists):
    slab_blocks = w_gate.shape[1] // WIDTH
    col_id = lax.axis_index("col").astype(jnp.int32).reshape(1)
    gate, up, down = pick(block_lists, col_id, w_gate, w_up, w_down)
    return layer(block_lists, activations, gate, up, down, rows, cols, slab_blocks)


def solution(mesh):
    rows, cols = mesh.shape["row"], mesh.shape["col"]
    near = rows == 4 and cols == 4
    body = functools.partial(near_shards, rows, cols) if near else general_shards
    in_specs = (
        P(("groups", "row"), "col"),
        P("row", "col"),
        P("row", "col"),
        P("row", "col"),
        P("groups", None, None),
    )
    out_specs = P(("groups", "row"), "col")
    return jax.shard_map(body, mesh=mesh, in_specs=in_specs, out_specs=out_specs, check_vma=False)
```

```python
import functools

import jax
import jax.numpy as jnp
from jax import lax
from jax.experimental import pallas as pl
from jax.experimental.pallas import tpu as pltpu
from jax.sharding import PartitionSpec as P

WIDTH = 128
PARTS = 2


def partner_2(block, axis, stride):
    count = lax.axis_size(axis)
    route = []
    for low in range(count):
        high = low | 1 << stride
        if high != low and high < count:
            route += [(low, high), (high, low)]
    return lax.ppermute(block, axis, route)


def general_shards(activations, w_gate, w_up, w_down, block_lists):
    row_count = lax.axis_size("row")
    row_id = lax.axis_index("row")
    col_id = lax.axis_index("col")
    slab_blocks = w_gate.shape[1] // WIDTH
    gathered = lax.all_gather(activations, "col", axis=1, tiled=True)
    partner = partner_2(gathered, "row", 0)
    wanted = lax.dynamic_index_in_dim(block_lists, col_id, axis=1, keepdims=False).reshape(
        row_count
    )
    chosen = jnp.minimum(wanted, slab_blocks - 1)
    own_entry = lax.dynamic_index_in_dim(wanted, row_id, axis=0, keepdims=False)
    live_flag = (own_entry < slab_blocks).astype(jnp.float32)

    def fetch(weight):
        pieces = weight.reshape(weight.shape[0], slab_blocks, WIDTH)
        outgoing = jnp.take(pieces, chosen, axis=1)
        got = lax.all_to_all(outgoing, "row", split_axis=1, concat_axis=0, tiled=True)
        return got.reshape(got.shape[0], WIDTH)

    gate_cols, up_cols, down_cols = fetch(w_gate), fetch(w_up), fetch(w_down)

    def term_of(token_rows):
        gate_value = jnp.dot(token_rows, gate_cols, preferred_element_type=jnp.float32)
        up_value = jnp.dot(token_rows, up_cols, preferred_element_type=jnp.float32)
        hidden = (jax.nn.relu(gate_value) * up_value * live_flag).astype(jnp.bfloat16)
        return lax.dot_general(
            hidden, down_cols, (((1,), (1,)), ((), ())), preferred_element_type=jnp.float32
        ).astype(jnp.bfloat16)

    own = term_of(gathered)
    received = partner_2(term_of(partner), "row", 0)
    own_sum, other_sum = (
        lax.psum_scatter(term, "col", scatter_dimension=1, tiled=True).astype(jnp.float32)
        for term in (own, received)
    )
    return (own_sum + other_sum).astype(jnp.bfloat16)


def layer_kernel(
    slab_blocks, lists, act, w_gate, w_up, w_down, out,
    gate_w, up_w, down_w, x_all, part_f32, part_out, part_in, hid_all,
    term, term_in, half_out, half_in, sum_out,
    w_sem, a_send, a_recv, g1_send, g1_recv, g2_send, g2_recv, g3_send, g3_recv,
    p_send, p_recv, h_send, h_recv, t_send, t_recv, s_send, s_recv, o_send, o_recv,
):
    parts, rows, cols, size, depth = x_all.shape
    blocks = rows // 2
    toks = cols * size
    r, c = lax.axis_index("row"), lax.axis_index("col")
    core, chip = c % 2, c // 2
    c1 = c + 1 - 2 * core
    c2 = (c + 2) % 4
    c3 = (c1 + 2) % 4

    def load(source, target, sem):
        for block in range(slab_blocks + 1):
            at = min(block, slab_blocks - 1) * WIDTH
            pltpu.make_async_copy(source.at[:, pl.ds(at, WIDTH)], target.at[block], sem).start()

    def loaded(target, sem):
        pltpu.make_async_copy(target, target, sem).wait()

    barrier = pltpu.get_barrier_semaphore()
    for dr in range(rows):
        for dc in range(cols):
            if dr or dc:
                pl.semaphore_signal(
                    barrier, inc=1,
                    device_id={"row": (r + dr) % rows, "col": (c + dc) % cols},
                    device_id_type=pl.DeviceIdType.MESH,
                )
    pl.semaphore_wait(barrier, rows * cols - 1)

    drains = []

    def remote(src, dst, send, recv, row, col):
        return pltpu.make_async_remote_copy(
            src_ref=src, dst_ref=dst, send_sem=send, recv_sem=recv,
            device_id={"row": row, "col": col}, device_id_type=pl.DeviceIdType.MESH,
        )

    def send_to(src, dst, send, recv, row, col):
        copy = remote(src, dst, send, recv, row, col)
        copy.start()
        drains.append((None, copy))

    def send_or_keep(src, dst, send, recv, row, col):
        other = jnp.logical_or(row != r, col != c)
        copy = remote(src, dst, send, recv, row, col)

        @pl.when(other)
        def _():
            copy.start()

        @pl.when(jnp.logical_not(other))
        def _():
            pltpu.make_async_copy(src, dst, recv).start()

        drains.append((other, copy))

    def arrived(dst, recv):
        pltpu.make_async_copy(dst, dst, recv).wait()

    def spread(p):
        for q in range(cols):
            send_or_keep(
                act.at[pl.ds((p * cols + q) * size, size)], x_all.at[p, r, q],
                a_send.at[p, q], a_recv.at[p, r], c, q,
            )

    def forward(p):
        for k in range(rows):
            s = (r + k) % rows
            piece = x_all.at[p, s, c]
            arrived(piece, a_recv.at[p, s])
            send_to(piece, piece, g2_send.at[p, k], g2_recv.at[p, s], r, c2)
            send_to(piece, piece, g1_send.at[p, k], g1_recv.at[p, s], r, c1)

    def forward_again(p):
        for k in range(rows):
            s = (r + k) % rows
            piece = x_all.at[p, s, c2]
            arrived(piece, g2_recv.at[p, s])
            send_to(piece, piece, g3_send.at[p, k], g3_recv.at[p, s], r, c1)

    def collected(p):
        for s in range(rows):
            arrived(x_all.at[p, s, c1], g1_recv.at[p, s])
        for s in range(rows):
            arrived(x_all.at[p, s, c3], g3_recv.at[p, s])

    def gate_up(p):
        for b in range(blocks):
            x = x_all[p, 2 * b : 2 * b + 2].reshape(2 * toks, depth)
            for j in range(2):
                block = lists[b, c, j]
                weight = jnp.concatenate([gate_w[block], up_w[block]], axis=1)
                value = jnp.dot(x, weight, preferred_element_type=jnp.float32)
                value = value.reshape(2, toks, 2 * WIDTH)
                lanes = slice(j * 2 * WIDTH, (j + 1) * 2 * WIDTH)
                part_f32[p, 2 * b : 2 * b + 2, :, lanes] = value
                part_out[p, 2 * b : 2 * b + 2, :, lanes] = value.astype(jnp.bfloat16)
        for k in range(1, rows):
            s = (r + k) % rows
            send_to(part_out.at[p, s], part_in.at[p, k - 1], p_send.at[p, k], p_recv.at[p, k], s, c)

    def hidden(p):
        total = part_f32[p, r]
        for k in range(1, rows):
            arrived(part_in.at[p, k - 1], p_recv.at[p, k])
            total = total + part_in[p, k - 1].astype(jnp.float32)
        for j in range(2):
            at = 2 * j * WIDTH
            live = jnp.where(lists[r // 2, c, j] < slab_blocks, 1.0, 0.0)
            value = jnp.maximum(total[:, at : at + WIDTH], 0.0) * total[:, at + WIDTH : at + 2 * WIDTH]
            hid_all[p, r, :, j * WIDTH : (j + 1) * WIDTH] = (value * live).astype(jnp.bfloat16)
        for k in range(1, rows):
            mine = hid_all.at[p, r]
            send_to(mine, mine, h_send.at[p, k], h_recv.at[p, k], (r + k) % rows, c)

    def down(p):
        for k in range(1, rows):
            arrived(hid_all.at[p, (r + rows - k) % rows], h_recv.at[p, k])
        tile = 512
        for b in range(blocks):
            h = hid_all[p, 2 * b : 2 * b + 2].reshape(2 * toks, 2 * WIDTH)
            for n in range(0, depth, tile):
                weight = jnp.concatenate(
                    [down_w[lists[b, c, j], n : n + tile] for j in range(2)], axis=1
                )
                value = lax.dot_general(
                    h, weight, (((1,), (1,)), ((), ())),
                    preferred_element_type=jnp.float32,
                ).astype(jnp.bfloat16)
                for i in range(2):
                    for q in range(cols):
                        at = (i * cols + q) * size
                        term[p, q % 2, q // 2, 2 * b + i, :, n : n + tile] = value[at : at + size]
        send_to(term.at[p, 1 - core], term_in.at[p], t_send.at[p], t_recv.at[p], r, c1)

    def pair(p):
        arrived(term_in.at[p], t_recv.at[p])
        for k in range(rows):
            s = (r + k) % rows
            value = term[p, core, 1 - chip, s].astype(jnp.float32)
            value = value + term_in[p, 1 - chip, s].astype(jnp.float32)
            half_out[p, s] = value.astype(jnp.bfloat16)
            send_to(half_out.at[p, s], half_in.at[p, s], s_send.at[p, k], s_recv.at[p, s], r, c2)

    def finish(p):
        for k in range(rows):
            s = (r + k) % rows
            value = term[p, core, chip, s].astype(jnp.float32)
            value = value + term_in[p, chip, s].astype(jnp.float32)
            arrived(half_in.at[p, s], s_recv.at[p, s])
            value = value + half_in[p, s].astype(jnp.float32)
            sum_out[p, s] = value.astype(jnp.bfloat16)
            send_or_keep(
                sum_out.at[p, s], out.at[pl.ds((p * cols + c) * size, size)],
                o_send.at[p, k], o_recv.at[p, c], s, r,
            )

    for p in range(parts):
        spread(p)
    load(w_gate, gate_w, w_sem.at[0])
    load(w_up, up_w, w_sem.at[1])
    load(w_down, down_w, w_sem.at[2])
    forward(0)
    forward_again(0)
    forward(1)
    collected(0)
    loaded(gate_w, w_sem.at[0])
    loaded(up_w, w_sem.at[1])
    gate_up(0)
    forward_again(1)
    collected(1)
    gate_up(1)
    hidden(0)
    loaded(down_w, w_sem.at[2])
    down(0)
    hidden(1)
    pair(0)
    down(1)
    finish(0)
    pair(1)
    finish(1)
    for p in range(parts):
        for q in range(cols):
            arrived(out.at[pl.ds((p * cols + q) * size, size)], o_recv.at[p, q])
    for other, copy in drains:
        if other is None:
            copy.wait_send()
        else:
            pl.when(other)(copy.wait_send)


def layer(block_lists, activations, gate, up, down, rows, cols, slab_blocks):
    tokens, depth = activations.shape
    size = tokens // (PARTS * cols)
    toks = cols * size
    bf16, f32 = jnp.bfloat16, jnp.float32
    sem = pltpu.SemaphoreType.DMA
    slab = pltpu.VMEM((slab_blocks + 1, gate.shape[0], WIDTH), bf16)
    by_row, by_col = sem((PARTS, rows)), sem((PARTS, cols))
    return pl.pallas_call(
        functools.partial(layer_kernel, slab_blocks),
        out_shape=jax.ShapeDtypeStruct(activations.shape, bf16),
        in_specs=[pl.BlockSpec(memory_space=pltpu.SMEM)] + [pl.BlockSpec(memory_space=pl.ANY)] * 4,
        out_specs=pl.BlockSpec(memory_space=pltpu.VMEM),
        scratch_shapes=[
            slab, slab, slab,
            pltpu.VMEM((PARTS, rows, cols, size, depth), bf16),
            pltpu.VMEM((PARTS, rows, toks, 4 * WIDTH), f32),
            pltpu.VMEM((PARTS, rows, toks, 4 * WIDTH), bf16),
            pltpu.VMEM((PARTS, rows - 1, toks, 4 * WIDTH), bf16),
            pltpu.VMEM((PARTS, rows, toks, 2 * WIDTH), bf16),
            pltpu.VMEM((PARTS, 2, 2, rows, size, depth), bf16),
            pltpu.VMEM((PARTS, 2, rows, size, depth), bf16),
            pltpu.VMEM((PARTS, rows, size, depth), bf16),
            pltpu.VMEM((PARTS, rows, size, depth), bf16),
            pltpu.VMEM((PARTS, rows, size, depth), bf16),
            sem((3,)),
            by_col, by_row,
            by_row, by_row, by_row, by_row, by_row, by_row,
            by_row, by_row, by_row, by_row,
            sem((PARTS,)), sem((PARTS,)),
            by_row, by_row, by_row, by_col,
        ],
        compiler_params=pltpu.CompilerParams(
            collective_id=0, has_side_effects=True, vmem_limit_bytes=60 * 2**20
        ),
    )(block_lists, activations, gate, up, down)


def near_shards(rows, cols, activations, w_gate, w_up, w_down, block_lists):
    slab_blocks = w_gate.shape[1] // WIDTH
    return layer(block_lists, activations, w_gate, w_up, w_down, rows, cols, slab_blocks)


def solution(mesh):
    rows, cols = mesh.shape["row"], mesh.shape["col"]
    near = rows == 4 and cols == 4
    body = functools.partial(near_shards, rows, cols) if near else general_shards
    in_specs = (
        P(("groups", "row"), "col"),
        P("row", "col"),
        P("row", "col"),
        P("row", "col"),
        P("groups", None, None),
    )
    out_specs = P(("groups", "row"), "col")
    return jax.shard_map(body, mesh=mesh, in_specs=in_specs, out_specs=out_specs, check_vma=False)
```

```python
import functools

import jax
import jax.numpy as jnp
from jax import lax
from jax.experimental import pallas as pl
from jax.experimental.pallas import tpu as pltpu
from jax.sharding import PartitionSpec as P

WIDTH = 128
PARTS = 2


def partner_2(block, axis, stride):
    count = lax.axis_size(axis)
    route = []
    for low in range(count):
        high = low | 1 << stride
        if high != low and high < count:
            route += [(low, high), (high, low)]
    return lax.ppermute(block, axis, route)


def general_shards(activations, w_gate, w_up, w_down, block_lists):
    row_count = lax.axis_size("row")
    row_id = lax.axis_index("row")
    col_id = lax.axis_index("col")
    slab_blocks = w_gate.shape[1] // WIDTH
    gathered = lax.all_gather(activations, "col", axis=1, tiled=True)
    partner = partner_2(gathered, "row", 0)
    wanted = lax.dynamic_index_in_dim(block_lists, col_id, axis=1, keepdims=False).reshape(
        row_count
    )
    chosen = jnp.minimum(wanted, slab_blocks - 1)
    own_entry = lax.dynamic_index_in_dim(wanted, row_id, axis=0, keepdims=False)
    live_flag = (own_entry < slab_blocks).astype(jnp.float32)

    def fetch(weight):
        pieces = weight.reshape(weight.shape[0], slab_blocks, WIDTH)
        outgoing = jnp.take(pieces, chosen, axis=1)
        got = lax.all_to_all(outgoing, "row", split_axis=1, concat_axis=0, tiled=True)
        return got.reshape(got.shape[0], WIDTH)

    gate_cols, up_cols, down_cols = fetch(w_gate), fetch(w_up), fetch(w_down)

    def term_of(token_rows):
        gate_value = jnp.dot(token_rows, gate_cols, preferred_element_type=jnp.float32)
        up_value = jnp.dot(token_rows, up_cols, preferred_element_type=jnp.float32)
        hidden = (jax.nn.relu(gate_value) * up_value * live_flag).astype(jnp.bfloat16)
        return lax.dot_general(
            hidden, down_cols, (((1,), (1,)), ((), ())), preferred_element_type=jnp.float32
        ).astype(jnp.bfloat16)

    own = term_of(gathered)
    received = partner_2(term_of(partner), "row", 0)
    own_sum, other_sum = (
        lax.psum_scatter(term, "col", scatter_dimension=1, tiled=True).astype(jnp.float32)
        for term in (own, received)
    )
    return (own_sum + other_sum).astype(jnp.bfloat16)


def layer_kernel(
    slab_blocks, lists, act, w_gate, w_up, w_down, out,
    gate_w, up_w, down_w, x_cross, x_all, part_f32, part_out, part_in, hid_all,
    term, term_in, half_out, half_in, sum_out,
    w_sem, c_send, c_recv, a_send, a_recv, g1_send, g1_recv, g2_send, g2_recv, g3_send, g3_recv,
    p_send, p_recv, h_send, h_recv, t_send, t_recv, s_send, s_recv, o_send, o_recv,
):
    parts, rows, cols, size, depth = x_all.shape
    blocks = rows // 2
    toks = cols * size
    r, c = lax.axis_index("row"), lax.axis_index("col")
    core, chip = c % 2, c // 2
    c1 = c + 1 - 2 * core
    c2 = (c + 2) % 4
    c3 = (c1 + 2) % 4

    def load(source, target, sem):
        for block in range(slab_blocks + 1):
            at = min(block, slab_blocks - 1) * WIDTH
            pltpu.make_async_copy(source.at[:, pl.ds(at, WIDTH)], target.at[block], sem).start()

    def loaded(target, sem):
        pltpu.make_async_copy(target, target, sem).wait()

    barrier = pltpu.get_barrier_semaphore()
    for dr in range(rows):
        for dc in range(cols):
            if dr or dc:
                pl.semaphore_signal(
                    barrier, inc=1,
                    device_id={"row": (r + dr) % rows, "col": (c + dc) % cols},
                    device_id_type=pl.DeviceIdType.MESH,
                )
    pl.semaphore_wait(barrier, rows * cols - 1)

    drains = []

    def remote(src, dst, send, recv, row, col):
        return pltpu.make_async_remote_copy(
            src_ref=src, dst_ref=dst, send_sem=send, recv_sem=recv,
            device_id={"row": row, "col": col}, device_id_type=pl.DeviceIdType.MESH,
        )

    def send_to(src, dst, send, recv, row, col):
        copy = remote(src, dst, send, recv, row, col)
        copy.start()
        drains.append((None, copy))

    def send_or_keep(src, dst, send, recv, row, col):
        other = jnp.logical_or(row != r, col != c)
        copy = remote(src, dst, send, recv, row, col)

        @pl.when(other)
        def _():
            copy.start()

        @pl.when(jnp.logical_not(other))
        def _():
            pltpu.make_async_copy(src, dst, recv).start()

        drains.append((other, copy))

    def arrived(dst, recv):
        pltpu.make_async_copy(dst, dst, recv).wait()

    def cross(p):
        at = (p * cols + 2 * (1 - chip)) * size
        send_to(act.at[pl.ds(at, 2 * size)], x_cross.at[p], c_send.at[p], c_recv.at[p], r, c2)

    def spread_own(p):
        for j in range(2):
            q = 2 * chip + j
            send_or_keep(
                act.at[pl.ds((p * cols + q) * size, size)], x_all.at[p, r, q],
                a_send.at[p, j], a_recv.at[p, r], c, q,
            )

    def spread_other(p):
        arrived(x_cross.at[p], c_recv.at[p])
        for j in range(2):
            q = 2 * chip + j
            send_or_keep(
                x_cross.at[p, pl.ds(j * size, size)], x_all.at[p, r, q],
                a_send.at[p, 2 + j], a_recv.at[p, r], c2, q,
            )

    def forward(p):
        for k in range(rows):
            s = (r + k) % rows
            piece = x_all.at[p, s, c]
            arrived(piece, a_recv.at[p, s])
            send_to(piece, piece, g2_send.at[p, k], g2_recv.at[p, s], r, c2)
            send_to(piece, piece, g1_send.at[p, k], g1_recv.at[p, s], r, c1)

    def forward_again(p):
        for k in range(rows):
            s = (r + k) % rows
            piece = x_all.at[p, s, c2]
            arrived(piece, g2_recv.at[p, s])
            send_to(piece, piece, g3_send.at[p, k], g3_recv.at[p, s], r, c1)

    def collected(p):
        for s in range(rows):
            arrived(x_all.at[p, s, c1], g1_recv.at[p, s])
        for s in range(rows):
            arrived(x_all.at[p, s, c3], g3_recv.at[p, s])

    def gate_up(p):
        for b in range(blocks):
            x = x_all[p, 2 * b : 2 * b + 2].reshape(2 * toks, depth)
            for j in range(2):
                block = lists[b, c, j]
                weight = jnp.concatenate([gate_w[block], up_w[block]], axis=1)
                value = jnp.dot(x, weight, preferred_element_type=jnp.float32)
                value = value.reshape(2, toks, 2 * WIDTH)
                lanes = slice(j * 2 * WIDTH, (j + 1) * 2 * WIDTH)
                part_f32[p, 2 * b : 2 * b + 2, :, lanes] = value
                part_out[p, 2 * b : 2 * b + 2, :, lanes] = value.astype(jnp.bfloat16)
        for k in range(1, rows):
            s = (r + k) % rows
            send_to(part_out.at[p, s], part_in.at[p, k - 1], p_send.at[p, k], p_recv.at[p, k], s, c)

    def hidden(p):
        total = part_f32[p, r]
        for k in range(1, rows):
            arrived(part_in.at[p, k - 1], p_recv.at[p, k])
            total = total + part_in[p, k - 1].astype(jnp.float32)
        for j in range(2):
            at = 2 * j * WIDTH
            live = jnp.where(lists[r // 2, c, j] < slab_blocks, 1.0, 0.0)
            value = jnp.maximum(total[:, at : at + WIDTH], 0.0) * total[:, at + WIDTH : at + 2 * WIDTH]
            hid_all[p, r, :, j * WIDTH : (j + 1) * WIDTH] = (value * live).astype(jnp.bfloat16)
        for k in range(1, rows):
            mine = hid_all.at[p, r]
            send_to(mine, mine, h_send.at[p, k], h_recv.at[p, k], (r + k) % rows, c)

    def down(p):
        for k in range(1, rows):
            arrived(hid_all.at[p, (r + rows - k) % rows], h_recv.at[p, k])
        tile = 512
        for b in range(blocks):
            h = hid_all[p, 2 * b : 2 * b + 2].reshape(2 * toks, 2 * WIDTH)
            for n in range(0, depth, tile):
                weight = jnp.concatenate(
                    [down_w[lists[b, c, j], n : n + tile] for j in range(2)], axis=1
                )
                value = lax.dot_general(
                    h, weight, (((1,), (1,)), ((), ())),
                    preferred_element_type=jnp.float32,
                ).astype(jnp.bfloat16)
                for i in range(2):
                    for q in range(cols):
                        at = (i * cols + q) * size
                        term[p, q % 2, q // 2, 2 * b + i, :, n : n + tile] = value[at : at + size]
        send_to(term.at[p, 1 - core], term_in.at[p], t_send.at[p], t_recv.at[p], r, c1)

    def pair(p):
        arrived(term_in.at[p], t_recv.at[p])
        for k in range(rows):
            s = (r + k) % rows
            value = term[p, core, 1 - chip, s].astype(jnp.float32)
            value = value + term_in[p, 1 - chip, s].astype(jnp.float32)
            half_out[p, s] = value.astype(jnp.bfloat16)
            send_to(half_out.at[p, s], half_in.at[p, s], s_send.at[p, k], s_recv.at[p, s], r, c2)

    def finish(p):
        for k in range(rows):
            s = (r + k) % rows
            value = term[p, core, chip, s].astype(jnp.float32)
            value = value + term_in[p, chip, s].astype(jnp.float32)
            arrived(half_in.at[p, s], s_recv.at[p, s])
            value = value + half_in[p, s].astype(jnp.float32)
            sum_out[p, s] = value.astype(jnp.bfloat16)
            send_or_keep(
                sum_out.at[p, s], out.at[pl.ds((p * cols + c) * size, size)],
                o_send.at[p, k], o_recv.at[p, c], s, r,
            )

    for p in range(parts):
        cross(p)
        spread_own(p)
    load(w_gate, gate_w, w_sem.at[0])
    load(w_up, up_w, w_sem.at[1])
    load(w_down, down_w, w_sem.at[2])
    spread_other(0)
    spread_other(1)
    forward(0)
    forward(1)
    forward_again(0)
    collected(0)
    loaded(gate_w, w_sem.at[0])
    loaded(up_w, w_sem.at[1])
    loaded(down_w, w_sem.at[2])
    gate_up(0)
    forward_again(1)
    collected(1)
    gate_up(1)
    hidden(0)
    hidden(1)
    down(0)
    pair(0)
    down(1)
    pair(1)
    finish(0)
    finish(1)
    for p in range(parts):
        for q in range(cols):
            arrived(out.at[pl.ds((p * cols + q) * size, size)], o_recv.at[p, q])
    for other, copy in drains:
        if other is None:
            copy.wait_send()
        else:
            pl.when(other)(copy.wait_send)


def layer(block_lists, activations, gate, up, down, rows, cols, slab_blocks):
    tokens, depth = activations.shape
    size = tokens // (PARTS * cols)
    toks = cols * size
    bf16, f32 = jnp.bfloat16, jnp.float32
    sem = pltpu.SemaphoreType.DMA
    slab = pltpu.VMEM((slab_blocks + 1, gate.shape[0], WIDTH), bf16)
    by_row, by_col = sem((PARTS, rows)), sem((PARTS, cols))
    return pl.pallas_call(
        functools.partial(layer_kernel, slab_blocks),
        out_shape=jax.ShapeDtypeStruct(activations.shape, bf16),
        in_specs=[pl.BlockSpec(memory_space=pltpu.SMEM)] + [pl.BlockSpec(memory_space=pl.ANY)] * 4,
        out_specs=pl.BlockSpec(memory_space=pltpu.VMEM),
        scratch_shapes=[
            slab, slab, slab,
            pltpu.VMEM((PARTS, 2 * size, depth), bf16),
            pltpu.VMEM((PARTS, rows, cols, size, depth), bf16),
            pltpu.VMEM((PARTS, rows, toks, 4 * WIDTH), f32),
            pltpu.VMEM((PARTS, rows, toks, 4 * WIDTH), bf16),
            pltpu.VMEM((PARTS, rows - 1, toks, 4 * WIDTH), bf16),
            pltpu.VMEM((PARTS, rows, toks, 2 * WIDTH), bf16),
            pltpu.VMEM((PARTS, 2, 2, rows, size, depth), bf16),
            pltpu.VMEM((PARTS, 2, rows, size, depth), bf16),
            pltpu.VMEM((PARTS, rows, size, depth), bf16),
            pltpu.VMEM((PARTS, rows, size, depth), bf16),
            pltpu.VMEM((PARTS, rows, size, depth), bf16),
            sem((3,)),
            sem((PARTS,)), sem((PARTS,)),
            by_col, by_row,
            by_row, by_row, by_row, by_row, by_row, by_row,
            by_row, by_row, by_row, by_row,
            sem((PARTS,)), sem((PARTS,)),
            by_row, by_row, by_row, by_col,
        ],
        compiler_params=pltpu.CompilerParams(
            collective_id=0, has_side_effects=True, vmem_limit_bytes=60 * 2**20
        ),
    )(block_lists, activations, gate, up, down)


def near_shards(rows, cols, activations, w_gate, w_up, w_down, block_lists):
    slab_blocks = w_gate.shape[1] // WIDTH
    return layer(block_lists, activations, w_gate, w_up, w_down, rows, cols, slab_blocks)


def solution(mesh):
    rows, cols = mesh.shape["row"], mesh.shape["col"]
    near = rows == 4 and cols == 4
    body = functools.partial(near_shards, rows, cols) if near else general_shards
    in_specs = (
        P(("groups", "row"), "col"),
        P("row", "col"),
        P("row", "col"),
        P("row", "col"),
        P("groups", None, None),
    )
    out_specs = P(("groups", "row"), "col")
    return jax.shard_map(body, mesh=mesh, in_specs=in_specs, out_specs=out_specs, check_vma=False)
```

```python
import functools

import jax
import jax.numpy as jnp
from jax import lax
from jax.experimental import pallas as pl
from jax.experimental.pallas import tpu as pltpu
from jax.sharding import PartitionSpec as P

WIDTH = 128
PARTS = 2


def partner_2(block, axis, stride):
    count = lax.axis_size(axis)
    route = []
    for low in range(count):
        high = low | 1 << stride
        if high != low and high < count:
            route += [(low, high), (high, low)]
    return lax.ppermute(block, axis, route)


def general_shards(activations, w_gate, w_up, w_down, block_lists):
    row_count = lax.axis_size("row")
    row_id = lax.axis_index("row")
    col_id = lax.axis_index("col")
    slab_blocks = w_gate.shape[1] // WIDTH
    gathered = lax.all_gather(activations, "col", axis=1, tiled=True)
    partner = partner_2(gathered, "row", 0)
    wanted = lax.dynamic_index_in_dim(block_lists, col_id, axis=1, keepdims=False).reshape(
        row_count
    )
    chosen = jnp.minimum(wanted, slab_blocks - 1)
    own_entry = lax.dynamic_index_in_dim(wanted, row_id, axis=0, keepdims=False)
    live_flag = (own_entry < slab_blocks).astype(jnp.float32)

    def fetch(weight):
        pieces = weight.reshape(weight.shape[0], slab_blocks, WIDTH)
        outgoing = jnp.take(pieces, chosen, axis=1)
        got = lax.all_to_all(outgoing, "row", split_axis=1, concat_axis=0, tiled=True)
        return got.reshape(got.shape[0], WIDTH)

    gate_cols, up_cols, down_cols = fetch(w_gate), fetch(w_up), fetch(w_down)

    def term_of(token_rows):
        gate_value = jnp.dot(token_rows, gate_cols, preferred_element_type=jnp.float32)
        up_value = jnp.dot(token_rows, up_cols, preferred_element_type=jnp.float32)
        hidden = (jax.nn.relu(gate_value) * up_value * live_flag).astype(jnp.bfloat16)
        return lax.dot_general(
            hidden, down_cols, (((1,), (1,)), ((), ())), preferred_element_type=jnp.float32
        ).astype(jnp.bfloat16)

    own = term_of(gathered)
    received = partner_2(term_of(partner), "row", 0)
    own_sum, other_sum = (
        lax.psum_scatter(term, "col", scatter_dimension=1, tiled=True).astype(jnp.float32)
        for term in (own, received)
    )
    return (own_sum + other_sum).astype(jnp.bfloat16)


def layer_kernel(
    slab_blocks, lists, act, w_gate, w_up, w_down, out,
    gate_w, up_w, down_w, x_cross, x_all, part_f32, part_out, part_in, hid_all,
    term, term_in, half_out, half_in, sum_out,
    w_sem, c_send, c_recv, a_send, a_recv, g1_send, g1_recv, g2_send, g2_recv, g3_send, g3_recv,
    p_send, p_recv, h_send, h_recv, t_send, t_recv, s_send, s_recv, o_send, o_recv,
):
    parts, rows, cols, size, depth = x_all.shape
    blocks = rows // 2
    toks = cols * size
    r, c = lax.axis_index("row"), lax.axis_index("col")
    core, chip = c % 2, c // 2
    c1 = c + 1 - 2 * core
    c2 = (c + 2) % 4
    c3 = (c1 + 2) % 4

    def load(source, target, sem):
        for block in range(slab_blocks + 1):
            at = min(block, slab_blocks - 1) * WIDTH
            pltpu.make_async_copy(source.at[:, pl.ds(at, WIDTH)], target.at[block], sem).start()

    def loaded(target, sem):
        pltpu.make_async_copy(target, target, sem).wait()

    barrier = pltpu.get_barrier_semaphore()
    for dr in range(rows):
        for dc in range(cols):
            if dr or dc:
                pl.semaphore_signal(
                    barrier, inc=1,
                    device_id={"row": (r + dr) % rows, "col": (c + dc) % cols},
                    device_id_type=pl.DeviceIdType.MESH,
                )
    pl.semaphore_wait(barrier, rows * cols - 1)

    drains = []

    def remote(src, dst, send, recv, row, col):
        return pltpu.make_async_remote_copy(
            src_ref=src, dst_ref=dst, send_sem=send, recv_sem=recv,
            device_id={"row": row, "col": col}, device_id_type=pl.DeviceIdType.MESH,
        )

    def send_to(src, dst, send, recv, row, col):
        copy = remote(src, dst, send, recv, row, col)
        copy.start()
        drains.append((None, copy))

    def send_or_keep(src, dst, send, recv, row, col):
        other = jnp.logical_or(row != r, col != c)
        copy = remote(src, dst, send, recv, row, col)

        @pl.when(other)
        def _():
            copy.start()

        @pl.when(jnp.logical_not(other))
        def _():
            pltpu.make_async_copy(src, dst, recv).start()

        drains.append((other, copy))

    def arrived(dst, recv):
        pltpu.make_async_copy(dst, dst, recv).wait()

    def cross(p):
        at = (p * cols + 2 * (1 - chip)) * size
        send_to(act.at[pl.ds(at, 2 * size)], x_cross.at[p], c_send.at[p], c_recv.at[p], r, c2)

    def spread_own(p):
        for j in range(2):
            q = 2 * chip + j
            send_or_keep(
                act.at[pl.ds((p * cols + q) * size, size)], x_all.at[p, r, q],
                a_send.at[p, j], a_recv.at[p, r], c, q,
            )

    def spread_other(p):
        arrived(x_cross.at[p], c_recv.at[p])
        for j in range(2):
            q = 2 * chip + j
            send_or_keep(
                x_cross.at[p, pl.ds(j * size, size)], x_all.at[p, r, q],
                a_send.at[p, 2 + j], a_recv.at[p, r], c2, q,
            )

    def forward(p):
        for k in range(rows):
            s = (r + k) % rows
            piece = x_all.at[p, s, c]
            arrived(piece, a_recv.at[p, s])
            send_to(piece, piece, g2_send.at[p, k], g2_recv.at[p, s], r, c2)
            send_to(piece, piece, g1_send.at[p, k], g1_recv.at[p, s], r, c1)

    def forward_again(p):
        for k in range(rows):
            s = (r + k) % rows
            piece = x_all.at[p, s, c2]
            arrived(piece, g2_recv.at[p, s])
            send_to(piece, piece, g3_send.at[p, k], g3_recv.at[p, s], r, c1)

    def collected(p):
        for s in range(rows):
            arrived(x_all.at[p, s, c1], g1_recv.at[p, s])
        for s in range(rows):
            arrived(x_all.at[p, s, c3], g3_recv.at[p, s])

    def gate_up(p):
        for b in range(blocks):
            x = x_all[p, 2 * b : 2 * b + 2].reshape(2 * toks, depth)
            for j in range(2):
                block = lists[b, c, j]
                weight = jnp.concatenate([gate_w[block], up_w[block]], axis=1)
                value = jnp.dot(x, weight, preferred_element_type=jnp.float32)
                value = value.reshape(2, toks, 2 * WIDTH)
                lanes = slice(j * 2 * WIDTH, (j + 1) * 2 * WIDTH)
                part_f32[p, 2 * b : 2 * b + 2, :, lanes] = value
                part_out[p, 2 * b : 2 * b + 2, :, lanes] = value.astype(jnp.bfloat16)
            for s in (2 * b, 2 * b + 1):
                k = (s - r + rows) % rows
                copy = remote(
                    part_out.at[p, s], part_in.at[p, k], p_send.at[p, s], p_recv.at[p, k], s, c
                )
                pl.when(s != r)(copy.start)
                drains.append((s != r, copy))

    def hidden(p):
        total = part_f32[p, r]
        for k in range(1, rows):
            arrived(part_in.at[p, k], p_recv.at[p, k])
            total = total + part_in[p, k].astype(jnp.float32)
        for j in range(2):
            at = 2 * j * WIDTH
            live = jnp.where(lists[r // 2, c, j] < slab_blocks, 1.0, 0.0)
            value = jnp.maximum(total[:, at : at + WIDTH], 0.0) * total[:, at + WIDTH : at + 2 * WIDTH]
            hid_all[p, r, :, j * WIDTH : (j + 1) * WIDTH] = (value * live).astype(jnp.bfloat16)
        for k in range(1, rows):
            mine = hid_all.at[p, r]
            send_to(mine, mine, h_send.at[p, k], h_recv.at[p, k], (r + k) % rows, c)

    def down(p):
        for k in range(1, rows):
            arrived(hid_all.at[p, (r + rows - k) % rows], h_recv.at[p, k])
        tile = 512
        for b in range(blocks):
            h = hid_all[p, 2 * b : 2 * b + 2].reshape(2 * toks, 2 * WIDTH)
            for n in range(0, depth, tile):
                weight = jnp.concatenate(
                    [down_w[lists[b, c, j], n : n + tile] for j in range(2)], axis=1
                )
                value = lax.dot_general(
                    h, weight, (((1,), (1,)), ((), ())),
                    preferred_element_type=jnp.float32,
                ).astype(jnp.bfloat16)
                for i in range(2):
                    for q in range(cols):
                        at = (i * cols + q) * size
                        term[p, q % 2, q // 2, 2 * b + i, :, n : n + tile] = value[at : at + size]
        send_to(term.at[p, 1 - core], term_in.at[p], t_send.at[p], t_recv.at[p], r, c1)

    def pair(p):
        arrived(term_in.at[p], t_recv.at[p])
        for k in range(rows):
            s = (r + k) % rows
            value = term[p, core, 1 - chip, s].astype(jnp.float32)
            value = value + term_in[p, 1 - chip, s].astype(jnp.float32)
            half_out[p, s] = value.astype(jnp.bfloat16)
            send_to(half_out.at[p, s], half_in.at[p, s], s_send.at[p, k], s_recv.at[p, s], r, c2)

    def finish(p):
        for k in range(rows):
            s = (r + k) % rows
            value = term[p, core, chip, s].astype(jnp.float32)
            value = value + term_in[p, chip, s].astype(jnp.float32)
            arrived(half_in.at[p, s], s_recv.at[p, s])
            value = value + half_in[p, s].astype(jnp.float32)
            sum_out[p, s] = value.astype(jnp.bfloat16)
            send_or_keep(
                sum_out.at[p, s], out.at[pl.ds((p * cols + c) * size, size)],
                o_send.at[p, k], o_recv.at[p, c], s, r,
            )

    cross(0)
    spread_own(0)
    cross(1)
    spread_other(0)
    spread_own(1)
    load(w_gate, gate_w, w_sem.at[0])
    load(w_up, up_w, w_sem.at[1])
    load(w_down, down_w, w_sem.at[2])
    forward(0)
    spread_other(1)
    forward_again(0)
    forward(1)
    collected(0)
    loaded(gate_w, w_sem.at[0])
    loaded(up_w, w_sem.at[1])
    gate_up(0)
    forward_again(1)
    collected(1)
    gate_up(1)
    loaded(down_w, w_sem.at[2])
    hidden(0)
    hidden(1)
    down(0)
    pair(0)
    down(1)
    pair(1)
    finish(0)
    finish(1)
    for p in range(parts):
        for q in range(cols):
            arrived(out.at[pl.ds((p * cols + q) * size, size)], o_recv.at[p, q])
    for other, copy in drains:
        if other is None:
            copy.wait_send()
        else:
            pl.when(other)(copy.wait_send)


def layer(block_lists, activations, gate, up, down, rows, cols, slab_blocks):
    tokens, depth = activations.shape
    size = tokens // (PARTS * cols)
    toks = cols * size
    bf16, f32 = jnp.bfloat16, jnp.float32
    sem = pltpu.SemaphoreType.DMA
    slab = pltpu.VMEM((slab_blocks + 1, gate.shape[0], WIDTH), bf16)
    by_row, by_col = sem((PARTS, rows)), sem((PARTS, cols))
    return pl.pallas_call(
        functools.partial(layer_kernel, slab_blocks),
        out_shape=jax.ShapeDtypeStruct(activations.shape, bf16),
        in_specs=[pl.BlockSpec(memory_space=pltpu.SMEM)] + [pl.BlockSpec(memory_space=pl.ANY)] * 4,
        out_specs=pl.BlockSpec(memory_space=pltpu.VMEM),
        scratch_shapes=[
            slab, slab, slab,
            pltpu.VMEM((PARTS, 2 * size, depth), bf16),
            pltpu.VMEM((PARTS, rows, cols, size, depth), bf16),
            pltpu.VMEM((PARTS, rows, toks, 4 * WIDTH), f32),
            pltpu.VMEM((PARTS, rows, toks, 4 * WIDTH), bf16),
            pltpu.VMEM((PARTS, rows, toks, 4 * WIDTH), bf16),
            pltpu.VMEM((PARTS, rows, toks, 2 * WIDTH), bf16),
            pltpu.VMEM((PARTS, 2, 2, rows, size, depth), bf16),
            pltpu.VMEM((PARTS, 2, rows, size, depth), bf16),
            pltpu.VMEM((PARTS, rows, size, depth), bf16),
            pltpu.VMEM((PARTS, rows, size, depth), bf16),
            pltpu.VMEM((PARTS, rows, size, depth), bf16),
            sem((3,)),
            sem((PARTS,)), sem((PARTS,)),
            by_col, by_row,
            by_row, by_row, by_row, by_row, by_row, by_row,
            by_row, by_row, by_row, by_row,
            sem((PARTS,)), sem((PARTS,)),
            by_row, by_row, by_row, by_col,
        ],
        compiler_params=pltpu.CompilerParams(
            collective_id=0, has_side_effects=True, vmem_limit_bytes=60 * 2**20
        ),
    )(block_lists, activations, gate, up, down)


def near_shards(rows, cols, activations, w_gate, w_up, w_down, block_lists):
    slab_blocks = w_gate.shape[1] // WIDTH
    return layer(block_lists, activations, w_gate, w_up, w_down, rows, cols, slab_blocks)


def solution(mesh):
    rows, cols = mesh.shape["row"], mesh.shape["col"]
    near = rows == 4 and cols == 4
    body = functools.partial(near_shards, rows, cols) if near else general_shards
    in_specs = (
        P(("groups", "row"), "col"),
        P("row", "col"),
        P("row", "col"),
        P("row", "col"),
        P("groups", None, None),
    )
    out_specs = P(("groups", "row"), "col")
    return jax.shard_map(body, mesh=mesh, in_specs=in_specs, out_specs=out_specs, check_vma=False)
```
